256 devices in a mesh: ang: 32 (over y, z), rad: 8 (over x, core).
Axes of the slice: x: 4, y: 4, z: 8, core: 2. Of those that a mesh axis runs over, the one named last changes fastest.
Arguments:
- grid_field: bfloat16 [2, 128, 768, 1536], P(None, 'rad', 'ang'), may hold values from -6 to 6
- slot_order: int32 [512], replicated, may hold values from 0 to 511, as said below
- legendre: bfloat16 [512, 384, 512], P('ang'), may hold values from -0.21875 to 0.21875
- inverses: bfloat16 [512, 128, 128], P('rad'), may hold values from -0.2 to 1.7, as said below
Outputs:
- spectrum: float32 [2, 512, 2, 512, 128], P(None, 'ang', None, 'rad')
The draws below stay inside these ranges and needn't reach their ends.
Inputs may be any that keep to these rules, and one draw needn't show every extreme that they name: `slot_order`: slots 2 k and 2 k + 1 hold orders m and 511 - m; every order appears in exactly one slot. `inverses`: each degree's matrix is a diagonal part between 0.5 and 1.5 plus entries of zero mean and magnitude at most 0.19.
All inputs are finite; a program needn't handle non-finite values.
Results may differ from the reference program's by a relative error of at most 0.0057.
Values may be sent and summed in bfloat16 or wider, within the bound.
No kernel may reach another device: no remote copies, remote signals or barrier semaphores. Data moves between devices by JAX's collectives and lax.ppermute only.
A program may use at most 128 MiB of HBM per device.

```python
import math
import jax
import jax.numpy as jnp
from jax import lax

DEGREES = 512
LATS = 768
LONS = 1536
RADII = 128
FIELDS = 2


def draw_slot_order(key, part):
    key = jax.random.fold_in(key, 3)
    lower = jax.random.permutation(key, DEGREES // 2).astype(jnp.int32)
    upper = DEGREES - 1 - lower
    return jnp.stack([lower, upper], axis=1).reshape(DEGREES).astype(jnp.int32)


def draw_inverses(key, part):
    key = jax.random.fold_in(key, 7)
    noise_key, diag_key = jax.random.split(key)
    spread = 0.5 / math.sqrt(RADII)
    shape = (DEGREES, RADII, RADII)
    noise = jax.random.normal(noise_key, shape, jnp.float32) * spread
    noise = jnp.clip(noise, -0.19, 0.19)
    diagonal = jax.random.uniform(diag_key, (DEGREES, RADII, 1), jnp.float32, 0.5, 1.5)
    rows = radial_rows()
    identity = (rows[:, None] == rows[None, :]).astype(jnp.float32)
    return (noise + identity[None, :, :] * diagonal).astype(jnp.bfloat16)


def radial_rows():
    return jnp.arange(RADII, dtype=jnp.int32)


def block_scale(key, shape, pieces, low, largest):
    def one(dim, blocks):
        heights = jax.random.uniform(jax.random.fold_in(jax.random.fold_in(key, 6), dim), (blocks,), jnp.float32, low / len(pieces), largest / len(pieces))
        return jnp.repeat(jnp.exp(heights), shape[dim] // blocks).reshape((-1,) + (1,) * (len(shape) - dim - 1))

    factor_of = one(*pieces[0])
    for cut in pieces[1:]:
        factor_of = factor_of * one(*cut)
    return factor_of


def gaussian(rng, shape, deviation, most, pieces=(), held_as=jnp.bfloat16):
    gain = block_scale(rng, shape, pieces, -0.22, 0.18) if pieces else 1.0
    values = jax.random.normal(rng, shape, jnp.float32) * deviation * gain
    return jnp.minimum(jnp.maximum(values, -most), most).astype(held_as)


def setup_inputs(seed: int = 0) -> dict:
    key_list = jax.random.split(jax.random.key(seed), 5)
    return {
        "grid_field": gaussian(key_list[0], (FIELDS, RADII, LATS, LONS), 1.0, 6.0, ((1, 8), (2, 32))),
        "slot_order": draw_slot_order(jax.random.fold_in(key_list[4], 71), 0),
        "legendre": gaussian(key_list[2], (DEGREES, LATS // 2, DEGREES), LATS ** -0.5, 0.21875, ((0, 32),)),
        "inverses": draw_inverses(jax.random.fold_in(key_list[4], 71), 0),
    }


def fourier_matrix(slot_order):
    longitude = jnp.arange(LONS, dtype=jnp.int32)
    phase = longitude[:, None] * slot_order[None, :].astype(jnp.int32) % LONS
    angle = phase.astype(jnp.float32) * (2.0 * math.pi / LONS)
    factor = 1.0 / math.sqrt(LONS)
    stacked = jnp.stack([jnp.cos(angle) * factor, -jnp.sin(angle) * factor], axis=1)
    return stacked.astype(jnp.bfloat16)

def reference(grid_field, slot_order, legendre, inverses):
    fourier_table = fourier_matrix(slot_order)
    flat_table = fourier_table.reshape(LONS, 2 * DEGREES)

    def one_field(field_rows):
        product = jnp.dot(field_rows.reshape(-1, LONS), flat_table, preferred_element_type=jnp.float32)
        return product.astype(jnp.bfloat16).reshape(RADII, LATS, 2, DEGREES)
    fourier = lax.map(one_field, grid_field)
    half = LATS // 2
    northern = fourier[:, :, :half].astype(jnp.float32)
    southern = fourier[:, :, half:][:, :, ::-1].astype(jnp.float32)
    symmetric = jnp.moveaxis((northern + southern).astype(jnp.bfloat16), -1, 0)
    antisymmetric = jnp.moveaxis((northern - southern).astype(jnp.bfloat16), -1, 0)
    inverse_wide = inverses.astype(jnp.float32)
    degree = jnp.arange(DEGREES, dtype=jnp.int32)

    def one_slot(items):
        sym_slot, anti_slot, table_slot, order = items
        table_wide = table_slot.astype(jnp.float32)
        even_part = jnp.einsum('frhk,hl->kfrl', sym_slot.astype(jnp.float32), table_wide)
        odd_part = jnp.einsum('frhk,hl->kfrl', anti_slot.astype(jnp.float32), table_wide)
        parity = (degree + order) % 2 == 0
        chosen = jnp.where(parity, even_part, odd_part)
        coefficients = jnp.where(degree >= order, chosen, jnp.zeros_like(chosen)).astype(jnp.bfloat16)
        return jnp.einsum('kfrl,lqr->kflq', coefficients.astype(jnp.float32), inverse_wide)
    result = lax.map(one_slot, (symmetric, antisymmetric, legendre, slot_order.astype(jnp.int32)))
    return jnp.moveaxis(result, 0, 1)
```

```python
import functools
import math

import jax
import jax.numpy as jnp
import numpy as np
from jax import lax
from jax.experimental import pallas as pl
from jax.experimental.pallas import tpu as pltpu
from jax.sharding import PartitionSpec as P

LONS = 1536
HALF_LONS = LONS // 2
ORDERS = 512
PAIRS = ORDERS // 2
F32 = jnp.float32
BF16 = jnp.bfloat16


def transform_tables():
    longitude = np.arange(HALF_LONS, dtype=np.int64)[:, None]
    even = 2 * np.arange(PAIRS, dtype=np.int64)[None, :]
    tables = []
    for order in (even, ORDERS - 1 - even):
        angle = (longitude * order % LONS) * (2.0 * math.pi / LONS)
        columns = np.concatenate([np.cos(angle), -np.sin(angle)], axis=1)
        tables.append((columns / math.sqrt(LONS)).astype(np.float32).astype(BF16))
    return tables


def fourier_kernel(lats, order_ref, south_ref, x_ref, even_ref, odd_ref, out_ref, product, turned):
    rows = x_ref.shape[0]
    columns = rows // lats
    for start in range(0, rows, 256):
        near = x_ref[start : start + 256, :HALF_LONS].astype(F32)
        far = x_ref[start : start + 256, HALF_LONS:].astype(F32)
        for parity, table in enumerate((even_ref, odd_ref)):
            mixed = (near - far if parity else near + far).astype(BF16)
            result = jnp.dot(mixed, table[...], preferred_element_type=F32)
            for part in range(4):
                product[parity * 4 + part, start : start + 256, :] = result[:, part * 128 : part * 128 + 128]
    south = south_ref[0]

    def turn(row, _):
        placed = jnp.where(south == 1, lats - 1 - row, row)
        for half in range(2):
            picked = [product[2 * part + half, pl.ds(row, columns, stride=lats), :] for part in range(4)]
            block = jnp.concatenate(picked, axis=0).T
            turned[pl.ds(half * 128 * lats + placed, 128, stride=lats), :] = block
        return 0

    lax.fori_loop(0, lats, turn, 0)

    def place(step, _):
        picked = []
        for offset in range(2):
            order = order_ref[step * 4 + offset * 2]
            pair = jnp.where(order % 2 == 0, order, ORDERS - 1 - order) // 2
            picked.append(turned[pl.ds(pl.multiple_of(pair * lats, 8), lats), :])
        at = pl.ds(pl.multiple_of(step * 2 * lats, 16), 2 * lats)
        out_ref[at, :] = jnp.concatenate(picked, axis=0).astype(BF16)
        return 0

    lax.fori_loop(0, PAIRS // 2, place, 0)


def fourier_stage(slot_order, south, rows, lats):
    even, odd = transform_tables()
    smem = pl.BlockSpec(memory_space=pltpu.SMEM)
    vmem = pl.BlockSpec(memory_space=pltpu.VMEM)
    return pl.pallas_call(
        functools.partial(fourier_kernel, lats),
        out_shape=jax.ShapeDtypeStruct((PAIRS * lats, 128), BF16),
        in_specs=[smem, smem, vmem, vmem, vmem],
        out_specs=vmem,
        scratch_shapes=[
            pltpu.VMEM((8, rows.shape[0], 128), F32),
            pltpu.VMEM((PAIRS * lats, 128), F32),
        ],
        compiler_params=pltpu.CompilerParams(vmem_limit_bytes=48 * 2**20),
        name="fourier",
    )(slot_order, south, rows, jnp.asarray(even), jnp.asarray(odd))


def legendre_kernel(lats, order_ref, recv_ref, table_ref, out_ref):
    sources, _, _ = recv_ref.shape
    half = sources // 2
    step = pl.program_id(0)
    degrees = table_ref.shape[2]
    degree = lax.broadcasted_iota(jnp.int32, (64, degrees), 1)
    for pair in range(2):
        rows = slice(pair * lats, (pair + 1) * lats)
        pieces = [recv_ref[source, :, :].astype(F32)[rows] for source in range(sources)]
        north = jnp.concatenate(pieces[:half], axis=0)
        mirrored = jnp.concatenate(pieces[half:][::-1], axis=0)
        symmetric = (north + mirrored).T.astype(BF16)
        antisymmetric = (north - mirrored).T.astype(BF16)
        first = order_ref[(step * 2 + pair) * 2]
        first_odd = first % 2
        chosen = []
        for parity in range(2):
            order = jnp.where(first_odd == parity, first, ORDERS - 1 - first)
            slot = pair * 2 + jnp.where(first_odd == parity, 0, 1)
            wanted = slice(parity * 64, parity * 64 + 64)
            both = jnp.concatenate([symmetric[wanted], antisymmetric[wanted]], axis=0)
            result = jnp.dot(both, table_ref[slot], preferred_element_type=F32)
            kept = jnp.where(degree % 2 == parity, result[:64], result[64:])
            chosen.append(jnp.where(degree >= order, kept, 0.0))
        for block in range(degrees // 64):
            lanes = slice(block * 64, block * 64 + 64)
            joined = jnp.concatenate([chosen[0][:, lanes], chosen[1][:, lanes]], axis=1)
            out_ref[block, pair * 64 : pair * 64 + 64, :] = joined.astype(BF16)


def legendre_stage(orders, received, legendre, lats):
    sources, rows, _ = received.shape
    pairs = rows // lats
    slots, northern, degrees = legendre.shape
    return pl.pallas_call(
        functools.partial(legendre_kernel, lats),
        out_shape=jax.ShapeDtypeStruct((degrees // 64, pairs * 64, 128), BF16),
        grid=(pairs // 2,),
        in_specs=[
            pl.BlockSpec(memory_space=pltpu.SMEM),
            pl.BlockSpec((sources, 2 * lats, 128), lambda step: (0, step, 0)),
            pl.BlockSpec((4, northern, degrees), lambda step: (step, 0, 0)),
        ],
        out_specs=pl.BlockSpec((degrees // 64, 128, 128), lambda step: (0, step, 0)),
        compiler_params=pltpu.CompilerParams(vmem_limit_bytes=48 * 2**20),
        name="legendre",
    )(orders, received, legendre)


def solve_kernel(order_ref, recv_ref, inverse_ref, out_ref, turned):
    sources, rows, _ = recv_ref.shape
    pairs = rows // 64
    degrees = inverse_ref.shape[0]
    lines = out_ref.shape[0] // degrees
    for pair in range(pairs):
        first_odd = order_ref[pair * 2] % 2
        for part in range(4):
            rows = slice(pair * 64 + part * 16, pair * 64 + part * 16 + 16)
            block = jnp.concatenate([recv_ref[source, rows, :] for source in range(sources)], axis=0)
            block = block.astype(F32).T
            for parity in range(2):
                slot = pair * 2 + jnp.where(first_odd == parity, 0, 1)
                line = (part // 2) * (4 * pairs) + slot * 2 + part % 2
                at = pl.ds(pl.multiple_of(line * degrees, 64), degrees)
                turned[at, :] = block[parity * 64 : parity * 64 + 64]

    def solve(degree, _):
        picked = turned[pl.ds(degree, lines, stride=degrees), :].astype(BF16)
        result = lax.dot_general(
            picked, inverse_ref[degree], (((1,), (1,)), ((), ())), preferred_element_type=F32
        )
        out_ref[pl.ds(degree, lines, stride=degrees), :] = result
        return 0

    lax.fori_loop(0, degrees, solve, 0, unroll=8)


def solve_stage(orders, received, inverses):
    sources, rows, _ = received.shape
    degrees = inverses.shape[0]
    lines = rows // 64 * 8
    smem = pl.BlockSpec(memory_space=pltpu.SMEM)
    vmem = pl.BlockSpec(memory_space=pltpu.VMEM)
    return pl.pallas_call(
        solve_kernel,
        out_shape=jax.ShapeDtypeStruct((lines * degrees, 128), F32),
        in_specs=[smem, vmem, vmem],
        out_specs=vmem,
        scratch_shapes=[pltpu.VMEM((lines * degrees, 128), F32)],
        compiler_params=pltpu.CompilerParams(vmem_limit_bytes=48 * 2**20),
        name="solve",
    )(orders, received, inverses)


def body(grid_field, slot_order, legendre, inverses):
    fields, radii, lats, lons = grid_field.shape
    slots = legendre.shape[0]
    place = lax.axis_index("ang")
    count = lax.axis_size("ang")
    south = (place >= count // 2).astype(jnp.int32).reshape(1)
    orders = lax.dynamic_slice_in_dim(slot_order, place * slots, slots)
    fourier = fourier_stage(slot_order, south, grid_field.reshape(fields * radii * lats, lons), lats)
    sent = fourier.reshape(count, slots // 2 * lats, 128)
    received = lax.all_to_all(sent, "ang", split_axis=0, concat_axis=0)
    coefficients = legendre_stage(orders, received, legendre, lats)
    moved = lax.all_to_all(coefficients, "rad", split_axis=0, concat_axis=0)
    spectrum = solve_stage(orders, moved, inverses)
    return spectrum.reshape(2, slots, fields, inverses.shape[0], 128)


def solution(mesh):
    placed = (P(None, "rad", "ang", None), P(), P("ang", None, None), P("rad", None, None))
    return jax.shard_map(
        body,
        mesh=mesh,
        in_specs=placed,
        out_specs=P(None, "ang", None, "rad", None),
        check_vma=False,
    )
```

```python
import functools
import math

import jax
import jax.numpy as jnp
import numpy as np
from jax import lax
from jax.experimental import pallas as pl
from jax.experimental.pallas import tpu as pltpu
from jax.sharding import PartitionSpec as P

LONS = 1536
HALF_LONS = LONS // 2
ORDERS = 512
PAIRS = ORDERS // 2
NA, NR = 32, 8
F32 = jnp.float32
BF16 = jnp.bfloat16
SMEM = pl.BlockSpec(memory_space=pltpu.SMEM)
VMEM = pl.BlockSpec(memory_space=pltpu.VMEM)
HBM = pl.BlockSpec(memory_space=pltpu.HBM)
PARAMS = pltpu.CompilerParams(vmem_limit_bytes=24 * 2**20)
ROWS = 256


def transform_tables():
    longitude = np.arange(HALF_LONS, dtype=np.int64)[:, None]
    even = 2 * np.arange(PAIRS, dtype=np.int64)[None, :]
    tables = []
    for order in (even, ORDERS - 1 - even):
        angle = (longitude * order % LONS) * (2.0 * math.pi / LONS)
        columns = np.concatenate([np.cos(angle), -np.sin(angle)], axis=1)
        tables.append((columns / math.sqrt(LONS)).astype(np.float32).astype(BF16))
    return np.stack(tables)


def fourier_kernel(lats, order_ref, x_hbm, table_hbm, out_ref, x_ref, table_ref, product, turned, sems):
    place = lax.axis_index("ang")
    rows = x_ref.shape[0]
    columns = rows // lats
    copies = []
    for parity in range(2):
        copies.append(pltpu.make_async_copy(table_hbm.at[parity], table_ref.at[parity], sems.at[parity]))
    for index, start in enumerate(range(0, rows, ROWS)):
        at = pl.ds(start, ROWS)
        copies.append(pltpu.make_async_copy(x_hbm.at[at], x_ref.at[at], sems.at[2 + index]))
    for copy in (copies[0], copies[2], copies[1], *copies[3:]):
        copy.start()
    for index, start in enumerate(range(0, rows, ROWS)):
        copies[2 + index].wait()
        near = x_ref[start : start + ROWS, :HALF_LONS].astype(F32)
        far = x_ref[start : start + ROWS, HALF_LONS:].astype(F32)
        for parity in range(2):
            if start == 0:
                copies[parity].wait()
            mixed = (near - far if parity else near + far).astype(BF16)
            result = jnp.dot(mixed, table_ref[parity], preferred_element_type=F32)
            for part in range(4):
                product[parity * 4 + part, start : start + ROWS, :] = result[:, part * 128 : part * 128 + 128]

    def turn(row, _):
        placed = jnp.where(place >= NA // 2, lats - 1 - row, row)
        for half in range(2):
            picked = [product[2 * part + half, pl.ds(row, columns, stride=lats), :] for part in range(4)]
            block = jnp.concatenate(picked, axis=0).T
            turned[pl.ds(half * 128 * lats + placed, 128, stride=lats), :] = block
        return 0

    lax.fori_loop(0, lats, turn, 0, unroll=8)
    pairs = PAIRS // NA

    def put(device, _):
        for local in range(0, pairs, 2):
            picked = []
            for offset in range(2):
                order = order_ref[(device * pairs + local + offset) * 2]
                pair = lax.shift_right_logical(order ^ ((order & 1) * (ORDERS - 1)), 1)
                picked.append(turned[pl.ds(pl.multiple_of(pair * lats, 8), lats), :])
            out_ref[device, local * lats : (local + 2) * lats, :] = jnp.concatenate(picked, axis=0).astype(BF16)
        return 0

    lax.fori_loop(0, NA, put, 0, unroll=2)


def fourier_stage(slot_order, rows, lats):
    table = transform_tables()
    return pl.pallas_call(
        functools.partial(fourier_kernel, lats),
        out_shape=jax.ShapeDtypeStruct((NA, PAIRS // NA * lats, 128), BF16),
        in_specs=[SMEM, HBM, HBM],
        out_specs=VMEM,
        scratch_shapes=[
            pltpu.VMEM(rows.shape, BF16),
            pltpu.VMEM(table.shape, BF16),
            pltpu.VMEM((8, rows.shape[0], 128), F32),
            pltpu.VMEM((PAIRS * lats, 128), F32),
            pltpu.SemaphoreType.DMA((2 + rows.shape[0] // ROWS,)),
        ],
        compiler_params=pltpu.CompilerParams(vmem_limit_bytes=60 * 2**20),
        name="fourier",
    )(slot_order, rows, jnp.asarray(table))


def legendre_kernel(lats, order_ref, table_ref, received, out_ref):
    place = lax.axis_index("ang")
    slots, _, degrees = table_ref.shape
    half = NA // 2
    degree = lax.broadcasted_iota(jnp.int32, (64, degrees), 1)

    def couple(step, _):
        at = pl.ds(pl.multiple_of(step * 2 * lats, 16), 2 * lats)
        pieces = [received[source, at, :].astype(F32) for source in range(2 * half)]
        for pair in range(2):
            rows = slice(pair * lats, (pair + 1) * lats)
            north = jnp.concatenate([piece[rows] for piece in pieces[:half]], axis=0)
            mirrored = jnp.concatenate([piece[rows] for piece in pieces[half:][::-1]], axis=0)
            symmetric = (north + mirrored).astype(BF16).T
            antisymmetric = (north - mirrored).astype(BF16).T
            first = step * 4 + pair * 2
            order_here = order_ref[place * slots + first]
            first_odd = order_here % 2
            chosen = []
            for parity in range(2):
                order = jnp.where(first_odd == parity, order_here, ORDERS - 1 - order_here)
                slot = first + jnp.where(first_odd == parity, 0, 1)
                wanted = slice(parity * 64, parity * 64 + 64)
                both = jnp.concatenate([symmetric[wanted], antisymmetric[wanted]], axis=0)
                result = jnp.dot(both, table_ref[slot], preferred_element_type=F32)
                kept = jnp.where(degree % 2 == parity, result[:64], result[64:])
                chosen.append(jnp.where(degree >= order, kept, 0.0).astype(BF16))
            out_at = pl.ds(pl.multiple_of(step * 128 + pair * 64, 64), 64)
            for block in range(NR):
                lanes = slice(block * 64, block * 64 + 64)
                joined = jnp.concatenate([chosen[0][:, lanes], chosen[1][:, lanes]], axis=1)
                out_ref[block, out_at, :] = joined
        return 0

    lax.fori_loop(0, slots // 4, couple, 0, unroll=4)


def legendre_stage(slot_order, received, legendre, lats):
    slots, _, degrees = legendre.shape
    return pl.pallas_call(
        functools.partial(legendre_kernel, lats),
        out_shape=jax.ShapeDtypeStruct((NR, slots * 32, 128), BF16),
        in_specs=[SMEM, VMEM, VMEM],
        out_specs=VMEM,
        compiler_params=PARAMS,
        name="legendre",
    )(slot_order, legendre, received)


def solve_kernel(order_ref, inverse_ref, received, out_hbm, turned, solved, sems):
    place = lax.axis_index("ang")
    degrees = inverse_ref.shape[0]
    lines = solved.shape[1]
    pairs = lines // 8
    for pair in range(pairs):
        first_odd = order_ref[(place * pairs + pair) * 2] & 1
        for part in range(4):
            at = slice(pair * 64 + part * 16, pair * 64 + part * 16 + 16)
            block = jnp.concatenate([received[source, at, :] for source in range(NR)], axis=0)
            block = block.astype(F32).T
            for parity in range(2):
                slot = pair * 2 + (first_odd ^ parity)
                line = (part // 2) * (4 * pairs) + slot * 2 + part % 2
                turned[pl.ds(pl.multiple_of(line * 64, 64), 64), :] = block[parity * 64 : parity * 64 + 64]

    def copy(group):
        at = pl.ds(pl.multiple_of(group * 8, 8), 8)
        return pltpu.make_async_copy(solved.at[group], out_hbm.at[:, at], sems.at[group])

    def solve(group, _):
        for degree in range(8):
            picked = turned[pl.ds(group * 8 + degree, lines, stride=64), :].astype(BF16)
            solved[group, :, degree, :] = lax.dot_general(
                picked, inverse_ref[group * 8 + degree], (((1,), (1,)), ((), ())), preferred_element_type=F32
            )
        copy(group).start()
        return 0

    lax.fori_loop(0, degrees // 8, solve, 0)
    for group in range(degrees // 8):
        copy(group).wait()


def solve_stage(slot_order, received, inverses):
    degrees = inverses.shape[0]
    lines = received.shape[1] // 8
    return pl.pallas_call(
        solve_kernel,
        out_shape=jax.ShapeDtypeStruct((lines, degrees, 128), F32),
        in_specs=[SMEM, VMEM, VMEM],
        out_specs=HBM,
        scratch_shapes=[
            pltpu.VMEM((lines * degrees, 128), F32),
            pltpu.VMEM((degrees // 8, lines, 8, 128), F32),
            pltpu.SemaphoreType.DMA((degrees // 8,)),
        ],
        compiler_params=PARAMS,
        name="solve",
    )(slot_order, inverses, received)


def body(grid_field, slot_order, legendre, inverses):
    fields, radii, lats, lons = grid_field.shape
    slots = legendre.shape[0]
    sent = fourier_stage(slot_order, grid_field.reshape(fields * radii * lats, lons), lats)
    received = lax.all_to_all(sent, "ang", split_axis=0, concat_axis=0)
    coefficients = legendre_stage(slot_order, received, legendre, lats)
    moved = lax.all_to_all(coefficients, "rad", split_axis=0, concat_axis=0)
    spectrum = solve_stage(slot_order, moved, inverses)
    return spectrum.reshape(2, slots, fields, inverses.shape[0], 128)


def solution(mesh):
    placed = (P(None, "rad", "ang", None), P(), P("ang", None, None), P("rad", None, None))
    return jax.shard_map(
        body,
        mesh=mesh,
        in_specs=placed,
        out_specs=P(None, "ang", None, "rad", None),
        check_vma=False,
    )
```

```python
import functools
import math

import jax
import jax.numpy as jnp
import numpy as np
from jax import lax
from jax.experimental import pallas as pl
from jax.experimental.pallas import tpu as pltpu
from jax.sharding import PartitionSpec as P

LONS = 1536
HALF_LONS = LONS // 2
ORDERS = 512
PAIRS = ORDERS // 2
NA, NR = 32, 8
NX, NC = 4, 2
PARTS = (8,)
F32 = jnp.float32
BF16 = jnp.bfloat16
SMEM = pl.BlockSpec(memory_space=pltpu.SMEM)
VMEM = pl.BlockSpec(memory_space=pltpu.VMEM)
HBM = pl.BlockSpec(memory_space=pltpu.HBM)
PARAMS = pltpu.CompilerParams(vmem_limit_bytes=24 * 2**20)
ROWS = 256


def transform_tables():
    longitude = np.arange(HALF_LONS, dtype=np.int64)[:, None]
    even = 2 * np.arange(PAIRS, dtype=np.int64)[None, :]
    tables = []
    for order in (even, ORDERS - 1 - even):
        angle = (longitude * order % LONS) * (2.0 * math.pi / LONS)
        columns = np.concatenate([np.cos(angle), -np.sin(angle)], axis=1)
        tables.append((columns / math.sqrt(LONS)).astype(np.float32).astype(BF16))
    return np.stack(tables)


def fourier_kernel(lats, order_ref, x_hbm, table_hbm, out_ref, x_ref, table_ref, product, turned, sems):
    place = lax.axis_index("ang")
    rows = x_ref.shape[0]
    columns = rows // lats
    copies = []
    for parity in range(2):
        copies.append(pltpu.make_async_copy(table_hbm.at[parity], table_ref.at[parity], sems.at[parity]))
    for index, start in enumerate(range(0, rows, ROWS)):
        at = pl.ds(start, ROWS)
        copies.append(pltpu.make_async_copy(x_hbm.at[at], x_ref.at[at], sems.at[2 + index]))
    for copy in (copies[0], copies[2], copies[1], *copies[3:]):
        copy.start()
    for index, start in enumerate(range(0, rows, ROWS)):
        copies[2 + index].wait()
        near = x_ref[start : start + ROWS, :HALF_LONS].astype(F32)
        far = x_ref[start : start + ROWS, HALF_LONS:].astype(F32)
        for parity in range(2):
            if start == 0:
                copies[parity].wait()
            mixed = (near - far if parity else near + far).astype(BF16)
            result = jnp.dot(mixed, table_ref[parity], preferred_element_type=F32)
            for part in range(4):
                product[parity * 4 + part, start : start + ROWS, :] = result[:, part * 128 : part * 128 + 128]

    def turn(row, _):
        placed = jnp.where(place >= NA // 2, lats - 1 - row, row)
        for half in range(2):
            picked = [product[2 * part + half, pl.ds(row, columns, stride=lats), :] for part in range(4)]
            block = jnp.concatenate(picked, axis=0).T
            turned[pl.ds(half * 128 * lats + placed, 128, stride=lats), :] = block
        return 0

    lax.fori_loop(0, lats, turn, 0, unroll=8)
    pairs = PAIRS // NA

    def put(device, _):
        for local in range(0, pairs, 2):
            picked = []
            for offset in range(2):
                order = order_ref[(device * pairs + local + offset) * 2]
                pair = lax.shift_right_logical(order ^ ((order & 1) * (ORDERS - 1)), 1)
                picked.append(turned[pl.ds(pl.multiple_of(pair * lats, 8), lats), :])
            out_ref[device, local * lats : (local + 2) * lats, :] = jnp.concatenate(picked, axis=0).astype(BF16)
        return 0

    lax.fori_loop(0, NA, put, 0, unroll=2)


def fourier_stage(slot_order, rows, lats):
    table = transform_tables()
    return pl.pallas_call(
        functools.partial(fourier_kernel, lats),
        out_shape=jax.ShapeDtypeStruct((NA, PAIRS // NA * lats, 128), BF16),
        in_specs=[SMEM, HBM, HBM],
        out_specs=VMEM,
        scratch_shapes=[
            pltpu.VMEM(rows.shape, BF16),
            pltpu.VMEM(table.shape, BF16),
            pltpu.VMEM((8, rows.shape[0], 128), F32),
            pltpu.VMEM((PAIRS * lats, 128), F32),
            pltpu.SemaphoreType.DMA((2 + rows.shape[0] // ROWS,)),
        ],
        compiler_params=pltpu.CompilerParams(vmem_limit_bytes=52 * 2**20),
        name="fourier",
    )(slot_order, rows, jnp.asarray(table))


def legendre_kernel(lats, order_ref, table_ref, received, *refs):
    outs, (sent, symmetric, antisymmetric) = refs[:-3], refs[-3:]
    place = lax.axis_index("ang")
    column = lax.axis_index("rad")
    here_x, here_c = column // NC, column % NC
    slots, _, degrees = table_ref.shape
    half = NA // 2
    degree = lax.broadcasted_iota(jnp.int32, (64, degrees), 1)

    def upper_first(pair):
        return lax.shift_right_logical(order_ref[place * slots + pair * 2], 8)

    for step in range(slots // 4):
        at = slice(step * 2 * lats, (step + 1) * 2 * lats)
        pieces = [received[source, at, :].astype(F32) for source in range(2 * half)]
        for pair in range(step * 2, step * 2 + 2):
            rows = slice(pair % 2 * lats, (pair % 2 + 1) * lats)
            north = jnp.concatenate([piece[rows] for piece in pieces[:half]], axis=0)
            mirrored = jnp.concatenate([piece[rows] for piece in pieces[half:][::-1]], axis=0)
            symmetric[pair] = (north + mirrored).astype(BF16).T
            antisymmetric[pair] = (north - mirrored).astype(BF16).T

    for pair in range(slots // 2):
        first = order_ref[place * slots + pair * 2]
        lower = jnp.where(first >= ORDERS // 2, ORDERS - 1 - first, first)
        chosen = []
        for which, order in enumerate((lower, ORDERS - 1 - lower)):
            begin = which * (degrees // 2)
            wanted = pl.ds(pl.multiple_of((order & 1) * 64, 64), 64)
            both = jnp.concatenate([symmetric[pair, wanted], antisymmetric[pair, wanted]], axis=0)
            result = jnp.dot(both, table_ref[pair * 2 + (upper_first(pair) ^ which), :, begin:], preferred_element_type=F32)
            here = degree[:, begin:]
            kept = jnp.where(((here ^ order) & 1) == 0, result[:64], result[64:])
            chosen.append(jnp.where(here >= order, kept, 0.0).astype(BF16))
        out_at = slice(pair * 64, pair * 64 + 64)
        for block in range(NR):
            left = chosen[0][:, block * 64 : block * 64 + 64]
            right = jnp.zeros_like(left)
            if block * 64 >= degrees // 2:
                right = chosen[1][:, block * 64 - degrees // 2 : block * 64 - degrees // 2 + 64]
            step_x = (block // NC - here_x) & (NX - 1)
            sent[step_x * NC + ((block % NC) ^ here_c), out_at, :] = jnp.concatenate([left, right], axis=1)
    start = 0
    for part in range(len(PARTS)):
        rows = slice(start, start + PARTS[part] * 64)
        for step_x in range(NX):
            for step_c in range(NC):
                outs[part * NX + step_x][step_c] = sent[step_x * NC + step_c, rows, :]
        start += PARTS[part] * 64


def legendre_stage(slot_order, received, legendre, lats):
    slots, _, _ = legendre.shape
    shapes = [jax.ShapeDtypeStruct((NC, pairs * 64, 128), BF16) for pairs in PARTS for _ in range(NX)]
    sent = pl.pallas_call(
        functools.partial(legendre_kernel, lats),
        out_shape=shapes,
        in_specs=[SMEM, VMEM, VMEM],
        out_specs=[VMEM] * len(shapes),
        scratch_shapes=[
            pltpu.VMEM((NR, slots * 32, 128), BF16),
            pltpu.VMEM((slots // 2, 128, legendre.shape[1]), BF16),
            pltpu.VMEM((slots // 2, 128, legendre.shape[1]), BF16),
        ],
        compiler_params=pltpu.CompilerParams(vmem_limit_bytes=24 * 2**20),
        name="legendre",
    )(slot_order, legendre, received)
    return [sent[part * NX : (part + 1) * NX] for part in range(len(PARTS))]


def solve_kernel(first_pair, order_ref, inverse_ref, *refs):
    mine, others, (out_hbm, received, turned, solved, sems) = refs[:NX], refs[NX : 2 * NX], refs[-5:]
    place = lax.axis_index("ang")
    column = lax.axis_index("rad")
    here_x, here_c = column // NC, column % NC
    degrees = inverse_ref.shape[0]
    lines = solved.shape[1]
    pairs = lines // 8
    for step_x in range(NX):
        source = ((here_x - step_x) & (NX - 1)) * NC + here_c
        received[source] = mine[step_x][0]
        received[source ^ 1] = others[step_x][...]
    for pair in range(pairs):
        upper_first = lax.shift_right_logical(order_ref[(place * sum(PARTS) + first_pair + pair) * 2], 8)
        for part in range(4):
            at = slice(pair * 64 + part * 16, pair * 64 + part * 16 + 16)
            block = jnp.concatenate([received[source, at, :] for source in range(NR)], axis=0)
            block = block.astype(F32).T
            for which in range(2):
                slot = pair * 2 + (upper_first ^ which)
                line = (part // 2) * (4 * pairs) + slot * 2 + part % 2
                turned[pl.ds(pl.multiple_of(line * 64, 64), 64), :] = block[which * 64 : which * 64 + 64]

    def copies(group):
        at = pl.ds(pl.multiple_of(group * 8, 8), 8)
        whole = out_hbm.shape[0] // 2
        return [
            pltpu.make_async_copy(
                solved.at[group, pl.ds(k * (lines // 2), lines // 2)],
                out_hbm.at[pl.ds(k * whole + first_pair * 4, lines // 2), at],
                sems.at[group, k],
            )
            for k in range(2)
        ]

    def solve(group, _):
        for degree in range(8):
            picked = turned[pl.ds(group * 8 + degree, lines, stride=64), :].astype(BF16)
            solved[group, :, degree, :] = lax.dot_general(
                picked, inverse_ref[group * 8 + degree], (((1,), (1,)), ((), ())), preferred_element_type=F32
            )
        for copy in copies(group):
            copy.start()
        return 0

    lax.fori_loop(0, degrees // 8, solve, 0, unroll=2)
    for group in range(degrees // 8):
        for copy in copies(group):
            copy.wait()


def solve_stage(slot_order, mine, others, inverses, first_pair, earlier):
    degrees = inverses.shape[0]
    lines = mine[0].shape[1] // 8
    operands = [slot_order, inverses, *mine, *others]
    specs = [SMEM] + [VMEM] * (len(operands) - 1)
    aliases = {}
    if earlier is not None:
        aliases = {len(operands): 0}
        operands.append(earlier)
        specs.append(HBM)
    return pl.pallas_call(
        functools.partial(solve_kernel, first_pair),
        out_shape=jax.ShapeDtypeStruct((sum(PARTS) * 8, degrees, 128), F32),
        in_specs=specs,
        out_specs=HBM,
        input_output_aliases=aliases,
        scratch_shapes=[
            pltpu.VMEM((NR, lines * 8, 128), BF16),
            pltpu.VMEM((lines * degrees, 128), F32),
            pltpu.VMEM((degrees // 8, lines, 8, 128), F32),
            pltpu.SemaphoreType.DMA((degrees // 8, 2)),
        ],
        compiler_params=PARAMS,
        name="solve",
    )(*operands)


def along_x(parts):
    moved = [None] * NX
    moved[0] = parts[0]
    for step in (2, 1, 3):
        moved[step] = lax.ppermute(
            parts[step], "rad", [(a, (a + step * NC) % (NX * NC)) for a in range(NX * NC)]
        )
    return moved


def along_core(parts):
    swap = [(a, a ^ 1) for a in range(NX * NC)]
    return [lax.ppermute(part[1], "rad", swap) for part in parts]


def body(grid_field, slot_order, legendre, inverses):
    fields, radii, lats, lons = grid_field.shape
    slots = legendre.shape[0]
    sent = fourier_stage(slot_order, grid_field.reshape(fields * radii * lats, lons), lats)
    received = lax.all_to_all(sent, "ang", split_axis=0, concat_axis=0)
    parts = [along_x(part) for part in legendre_stage(slot_order, received, legendre, lats)]
    spectrum, first = None, 0
    for part, pairs in zip(parts, PARTS):
        spectrum = solve_stage(slot_order, part, along_core(part), inverses, first, spectrum)
        first += pairs
    return spectrum.reshape(2, slots, fields, inverses.shape[0], 128)


def solution(mesh):
    placed = (P(None, "rad", "ang", None), P(), P("ang", None, None), P("rad", None, None))
    return jax.shard_map(
        body,
        mesh=mesh,
        in_specs=placed,
        out_specs=P(None, "ang", None, "rad", None),
        check_vma=False,
    )
```

```python
import functools
import math

import jax
import jax.numpy as jnp
import numpy as np
from jax import lax
from jax.experimental import pallas as pl
from jax.experimental.pallas import tpu as pltpu
from jax.sharding import PartitionSpec as P

LONS = 1536
HALF_LONS = LONS // 2
ORDERS = 512
PAIRS = ORDERS // 2
NA, NR = 32, 8
NX, NC = 4, 2
ARRIVALS = (0, 2, 1, 3)
DIRECT = (1, 3)
F32 = jnp.float32
BF16 = jnp.bfloat16
SMEM = pl.BlockSpec(memory_space=pltpu.SMEM)
VMEM = pl.BlockSpec(memory_space=pltpu.VMEM)
HBM = pl.BlockSpec(memory_space=pltpu.HBM)
PARAMS = pltpu.CompilerParams(vmem_limit_bytes=24 * 2**20)
ROWS = 256
LINE = 72


def transform_tables():
    longitude = np.arange(HALF_LONS, dtype=np.int64)[:, None]
    halves = []
    for pairs in np.split(np.arange(PAIRS, dtype=np.int64), 2):
        tables = []
        for order in (2 * pairs, ORDERS - 1 - 2 * pairs):
            angle = (longitude * order[None, :] % LONS) * (2.0 * math.pi / LONS)
            columns = np.concatenate([np.cos(angle), -np.sin(angle)], axis=1)
            tables.append((columns / math.sqrt(LONS)).astype(np.float32).astype(BF16))
        halves.append(np.stack(tables))
    return np.stack(halves)


def fourier_kernel(lats, order_hbm, x_hbm, table_hbm, out_ref, order_ref, x_ref, table_ref, mixed, low, high, turned, sems):
    place = lax.axis_index("ang")
    rows = x_ref.shape[0]
    columns = rows // lats
    pairs = PAIRS // NA
    starts = range(0, rows, ROWS)
    order_copy = pltpu.make_async_copy(order_hbm, order_ref, sems.at[0])
    x_copies = [
        pltpu.make_async_copy(x_hbm.at[pl.ds(start, ROWS)], x_ref.at[pl.ds(start, ROWS)], sems.at[1 + index])
        for index, start in enumerate(starts)
    ]
    table_copies = [
        [
            pltpu.make_async_copy(table_hbm.at[half, parity], table_ref.at[half, parity], sems.at[4 + half * 2 + parity])
            for parity in range(2)
        ]
        for half in range(2)
    ]
    for copy in (x_copies[0], *table_copies[0], *x_copies[1:], *table_copies[1], order_copy):
        copy.start()

    def turn(half, product, row):
        placed = jnp.where(place >= NA // 2, lats - 1 - row, row)
        picked = [product[part, pl.ds(row, columns, stride=lats), :] for part in range(4)]
        block = jnp.concatenate(picked, axis=0).T
        turned[pl.ds(half * 128 * lats + placed, 128, stride=lats), :] = block

    for index, start in enumerate(starts):
        x_copies[index].wait()
        near = x_ref[start : start + ROWS, :HALF_LONS].astype(F32)
        far = x_ref[start : start + ROWS, HALF_LONS:].astype(F32)
        mixed[0, start : start + ROWS, :] = (near + far).astype(BF16)
        mixed[1, start : start + ROWS, :] = (near - far).astype(BF16)
        for parity in range(2):
            if start == 0:
                table_copies[0][parity].wait()
            result = jnp.dot(mixed[parity, start : start + ROWS, :], table_ref[0, parity], preferred_element_type=F32)
            for part in range(2):
                low[parity * 2 + part, start : start + ROWS, :] = result[:, part * 128 : part * 128 + 128]
    for parity in range(2):
        table_copies[1][parity].wait()
    share = lats // 2
    for index in range(2):
        result = jnp.dot(mixed[index], table_ref[1, index], preferred_element_type=F32)
        for part in range(2):
            high[index * 2 + part] = result[:, part * 128 : part * 128 + 128]
        for row in range(index * share, (index + 1) * share):
            turn(0, low, row)

    def turn_high(row, _):
        turn(1, high, row)
        return 0

    lax.fori_loop(0, lats, turn_high, 0, unroll=8)
    order_copy.wait()

    def put(device, _):
        for local in range(0, pairs, 2):
            picked = []
            for offset in range(2):
                order = order_ref[(device * pairs + local + offset) * 2]
                pair = lax.shift_right_logical(order ^ ((order & 1) * (ORDERS - 1)), 1)
                picked.append(turned[pl.ds(pl.multiple_of(pair * lats, 8), lats), :])
            out_ref[device, local * lats : (local + 2) * lats, :] = jnp.concatenate(picked, axis=0).astype(BF16)
        return 0

    lax.fori_loop(0, NA, put, 0, unroll=2)


def fourier_stage(slot_order, rows, lats):
    table = transform_tables()
    count = rows.shape[0]
    return pl.pallas_call(
        functools.partial(fourier_kernel, lats),
        out_shape=jax.ShapeDtypeStruct((NA, PAIRS // NA * lats, 128), BF16),
        in_specs=[HBM, HBM, HBM],
        out_specs=VMEM,
        scratch_shapes=[
            pltpu.SMEM(slot_order.shape, jnp.int32),
            pltpu.VMEM(rows.shape, BF16),
            pltpu.VMEM(table.shape, BF16),
            pltpu.VMEM((2, count, HALF_LONS), BF16),
            pltpu.VMEM((4, count, 128), F32),
            pltpu.VMEM((4, count, 128), F32),
            pltpu.VMEM((PAIRS * lats, 128), F32),
            pltpu.SemaphoreType.DMA((8,)),
        ],
        compiler_params=pltpu.CompilerParams(vmem_limit_bytes=52 * 2**20),
        name="fourier",
    )(slot_order, rows, jnp.asarray(table))


def legendre_kernel(lats, order_ref, table_ref, received, *refs):
    outs, (sent, symmetric, antisymmetric) = refs[:-3], refs[-3:]
    place = lax.axis_index("ang")
    column = lax.axis_index("rad")
    here_x, here_c = column // NC, column % NC
    slots, _, degrees = table_ref.shape
    half = NA // 2
    degree = lax.broadcasted_iota(jnp.int32, (64, degrees), 1)

    def upper_first(pair):
        return lax.shift_right_logical(order_ref[place * slots + pair * 2], 8)

    for step in range(slots // 4):
        at = slice(step * 2 * lats, (step + 1) * 2 * lats)
        pieces = [received[source, at, :].astype(F32) for source in range(2 * half)]
        for pair in range(step * 2, step * 2 + 2):
            rows = slice(pair % 2 * lats, (pair % 2 + 1) * lats)
            north = jnp.concatenate([piece[rows] for piece in pieces[:half]], axis=0)
            mirrored = jnp.concatenate([piece[rows] for piece in pieces[half:][::-1]], axis=0)
            symmetric[pair] = (north + mirrored).astype(BF16).T
            antisymmetric[pair] = (north - mirrored).astype(BF16).T

    for pair in range(slots // 2):
        first = order_ref[place * slots + pair * 2]
        lower = jnp.where(first >= ORDERS // 2, ORDERS - 1 - first, first)
        chosen = []
        for which, order in enumerate((lower, ORDERS - 1 - lower)):
            begin = which * (degrees // 2)
            wanted = pl.ds(pl.multiple_of((order & 1) * 64, 64), 64)
            both = jnp.concatenate([symmetric[pair, wanted], antisymmetric[pair, wanted]], axis=0)
            result = jnp.dot(both, table_ref[pair * 2 + (upper_first(pair) ^ which), :, begin:], preferred_element_type=F32)
            here = degree[:, begin:]
            kept = jnp.where(((here ^ order) & 1) == 0, result[:64], result[64:])
            chosen.append(jnp.where(here >= order, kept, 0.0).astype(BF16))
        out_at = slice(pair * 64, pair * 64 + 64)
        for block in range(NR):
            left = chosen[0][:, block * 64 : block * 64 + 64]
            right = jnp.zeros_like(left)
            if block * 64 >= degrees // 2:
                right = chosen[1][:, block * 64 - degrees // 2 : block * 64 - degrees // 2 + 64]
            step_x = (block // NC - here_x) & (NX - 1)
            sent[step_x * NC + ((block % NC) ^ here_c), out_at, :] = jnp.concatenate([left, right], axis=1)
    outs = iter(outs)
    for step_x in range(NX):
        if step_x in DIRECT:
            for step_c in range(NC):
                next(outs)[...] = sent[step_x * NC + step_c]
        else:
            next(outs)[...] = sent[step_x * NC : step_x * NC + NC]


def legendre_stage(slot_order, received, legendre, lats):
    slots, _, _ = legendre.shape
    rows = slots * 32
    shapes = []
    for step_x in range(NX):
        if step_x in DIRECT:
            shapes += [jax.ShapeDtypeStruct((rows, 128), BF16)] * NC
        else:
            shapes.append(jax.ShapeDtypeStruct((NC, rows, 128), BF16))
    sent = pl.pallas_call(
        functools.partial(legendre_kernel, lats),
        out_shape=shapes,
        in_specs=[SMEM, VMEM, VMEM],
        out_specs=[VMEM] * len(shapes),
        scratch_shapes=[
            pltpu.VMEM((NR, slots * 32, 128), BF16),
            pltpu.VMEM((slots // 2, 128, legendre.shape[1]), BF16),
            pltpu.VMEM((slots // 2, 128, legendre.shape[1]), BF16),
        ],
        compiler_params=pltpu.CompilerParams(vmem_limit_bytes=24 * 2**20),
        name="legendre",
    )(slot_order, legendre, received)
    return sent


def solve_kernel(order_ref, inverse_ref, *refs):
    mine, others, (out_hbm, received, turned, solved, sems) = refs[:NX], refs[NX : 2 * NX], refs[-5:]
    place = lax.axis_index("ang")
    column = lax.axis_index("rad")
    here_x, here_c = column // NC, column % NC
    degrees = inverse_ref.shape[0]
    lines = solved.shape[1]
    pairs = lines // 8
    for index, step_x in enumerate(ARRIVALS):
        source = ((here_x - step_x) & (NX - 1)) * NC + here_c
        received[source] = mine[index][...] if step_x in DIRECT else mine[index][0]
        received[source ^ 1] = others[index][...]
    for pair in range(pairs):
        upper_first = lax.shift_right_logical(order_ref[(place * pairs + pair) * 2], 8)
        for part in range(4):
            at = slice(pair * 64 + part * 16, pair * 64 + part * 16 + 16)
            block = jnp.concatenate([received[source, at, :] for source in range(NR)], axis=0)
            block = block.astype(F32).T
            for which in range(2):
                slot = pair * 2 + (upper_first ^ which)
                line = (part // 2) * (4 * pairs) + slot * 2 + part % 2
                turned[pl.ds(pl.multiple_of(line * LINE, 8), 64), :] = block[which * 64 : which * 64 + 64]

    def copy(group):
        at = pl.ds(pl.multiple_of(group * 8, 8), 8)
        return pltpu.make_async_copy(solved.at[group], out_hbm.at[:, at], sems.at[group])

    def solve(group, _):
        for degree in range(8):
            picked = turned[pl.ds(group * 8 + degree, lines, stride=LINE), :].astype(BF16)
            solved[group, :, degree, :] = lax.dot_general(
                picked, inverse_ref[group * 8 + degree], (((1,), (1,)), ((), ())), preferred_element_type=F32
            )
        copy(group).start()
        return 0

    lax.fori_loop(0, degrees // 8, solve, 0, unroll=8)
    for group in range(degrees // 8):
        copy(group).wait()


def solve_stage(slot_order, mine, others, inverses):
    degrees = inverses.shape[0]
    lines = others[0].shape[0] // 8
    operands = [slot_order, inverses, *(mine[i] for i in ARRIVALS), *(others[i] for i in ARRIVALS)]
    return pl.pallas_call(
        solve_kernel,
        out_shape=jax.ShapeDtypeStruct((lines, degrees, 128), F32),
        in_specs=[SMEM] + [VMEM] * (len(operands) - 1),
        out_specs=HBM,
        scratch_shapes=[
            pltpu.VMEM((NR, lines * 8, 128), BF16),
            pltpu.VMEM((lines * LINE, 128), F32),
            pltpu.VMEM((degrees // 8, lines, 8, 128), F32),
            pltpu.SemaphoreType.DMA((degrees // 8,)),
        ],
        compiler_params=PARAMS,
        name="solve",
    )(*operands)


def along_rad(sent):
    def move(part, step_x, step_c):
        pairs = [(a, (a // NC + step_x) % NX * NC + (a % NC ^ step_c)) for a in range(NX * NC)]
        return lax.ppermute(part, "rad", pairs)

    sent = iter(sent)
    mine, others = [], []
    for step_x in range(NX):
        part = next(sent)
        if step_x in DIRECT:
            mine.append(move(part, step_x, 0))
            others.append(move(next(sent), step_x, 1))
        else:
            mine.append(move(part, step_x, 0) if step_x else part)
            others.append(move(mine[-1][1], 0, 1))
    return mine, others


def body(grid_field, slot_order, legendre, inverses):
    fields, radii, lats, lons = grid_field.shape
    slots = legendre.shape[0]
    sent = fourier_stage(slot_order, grid_field.reshape(fields * radii * lats, lons), lats)
    received = lax.all_to_all(sent, "ang", split_axis=0, concat_axis=0)
    mine, others = along_rad(legendre_stage(slot_order, received, legendre, lats))
    spectrum = solve_stage(slot_order, mine, others, inverses)
    return spectrum.reshape(2, slots, fields, inverses.shape[0], 128)


def solution(mesh):
    placed = (P(None, "rad", "ang", None), P(), P("ang", None, None), P("rad", None, None))
    return jax.shard_map(
        body,
        mesh=mesh,
        in_specs=placed,
        out_specs=P(None, "ang", None, "rad", None),
        check_vma=False,
    )
```

```python
import functools
import math

import jax
import jax.numpy as jnp
import numpy as np
from jax import lax
from jax.experimental import pallas as pl
from jax.experimental.pallas import tpu as pltpu
from jax.sharding import PartitionSpec as P

LONS = 1536
HALF_LONS = LONS // 2
ORDERS = 512
PAIRS = ORDERS // 2
NA, NR = 32, 8
NX, NC = 4, 2
ARRIVALS = (0, 2, 1, 3)
DIRECT = (1, 3)
F32 = jnp.float32
BF16 = jnp.bfloat16
SMEM = pl.BlockSpec(memory_space=pltpu.SMEM)
VMEM = pl.BlockSpec(memory_space=pltpu.VMEM)
HBM = pl.BlockSpec(memory_space=pltpu.HBM)
PARAMS = pltpu.CompilerParams(vmem_limit_bytes=24 * 2**20)
CUTS = ((0, 128), (128, 384), (384, 768))
LINE = 72


def transform_tables():
    longitude = np.arange(HALF_LONS, dtype=np.int64)[:, None]
    halves = []
    for pairs in np.split(np.arange(PAIRS, dtype=np.int64), 2):
        tables = []
        for order in (2 * pairs, ORDERS - 1 - 2 * pairs):
            angle = (longitude * order[None, :] % LONS) * (2.0 * math.pi / LONS)
            columns = np.concatenate([np.cos(angle), -np.sin(angle)], axis=1)
            tables.append((columns / math.sqrt(LONS)).astype(np.float32).astype(BF16))
        halves.append(np.stack(tables))
    return np.stack(halves)


def fourier_kernel(lats, order_hbm, x_hbm, table_hbm, out_ref, order_ref, x_ref, table_ref, mixed, low, high, turned, sems):
    place = lax.axis_index("ang")
    columns = x_ref.shape[0] // lats
    pairs = PAIRS // NA
    order_copy = pltpu.make_async_copy(order_hbm, order_ref, sems.at[0])
    x_copies = [
        pltpu.make_async_copy(x_hbm.at[start:stop], x_ref.at[start:stop], sems.at[1 + index])
        for index, (start, stop) in enumerate(CUTS)
    ]
    table_copies = [
        [
            pltpu.make_async_copy(table_hbm.at[half, parity], table_ref.at[half, parity], sems.at[4 + half * 2 + parity])
            for parity in range(2)
        ]
        for half in range(2)
    ]
    for copy in (x_copies[0], *table_copies[0], *x_copies[1:], *table_copies[1], order_copy):
        copy.start()

    def turn(half, product, row):
        placed = jnp.where(place >= NA // 2, lats - 1 - row, row)
        picked = [product[part, pl.ds(row, columns, stride=lats), :] for part in range(4)]
        block = jnp.concatenate(picked, axis=0).T
        turned[pl.ds(half * 128 * lats + placed, 128, stride=lats), :] = block

    for index, (start, stop) in enumerate(CUTS):
        x_copies[index].wait()
        near = x_ref[start:stop, :HALF_LONS].astype(F32)
        far = x_ref[start:stop, HALF_LONS:].astype(F32)
        mixed[0, start:stop, :] = (near + far).astype(BF16)
        mixed[1, start:stop, :] = (near - far).astype(BF16)
        for parity in range(2):
            if start == 0:
                table_copies[0][parity].wait()
            result = jnp.dot(mixed[parity, start:stop, :], table_ref[0, parity], preferred_element_type=F32)
            for part in range(2):
                low[parity * 2 + part, start:stop, :] = result[:, part * 128 : part * 128 + 128]
    for parity in range(2):
        table_copies[1][parity].wait()
    share = lats // 2
    for index in range(2):
        result = jnp.dot(mixed[index], table_ref[1, index], preferred_element_type=F32)
        for part in range(2):
            high[index * 2 + part] = result[:, part * 128 : part * 128 + 128]
        for row in range(index * share, (index + 1) * share):
            turn(0, low, row)

    def turn_high(row, _):
        turn(1, high, row)
        return 0

    lax.fori_loop(0, lats, turn_high, 0, unroll=24)
    order_copy.wait()

    def put(device, _):
        for local in range(0, pairs, 2):
            picked = []
            for offset in range(2):
                order = order_ref[(device * pairs + local + offset) * 2]
                pair = lax.shift_right_logical(order ^ ((order & 1) * (ORDERS - 1)), 1)
                picked.append(turned[pl.ds(pl.multiple_of(pair * lats, 8), lats), :])
            out_ref[device, local * lats : (local + 2) * lats, :] = jnp.concatenate(picked, axis=0).astype(BF16)
        return 0

    lax.fori_loop(0, NA, put, 0, unroll=8)


def fourier_stage(slot_order, rows, lats):
    table = transform_tables()
    count = rows.shape[0]
    return pl.pallas_call(
        functools.partial(fourier_kernel, lats),
        out_shape=jax.ShapeDtypeStruct((NA, PAIRS // NA * lats, 128), BF16),
        in_specs=[HBM, HBM, HBM],
        out_specs=VMEM,
        scratch_shapes=[
            pltpu.SMEM(slot_order.shape, jnp.int32),
            pltpu.VMEM(rows.shape, BF16),
            pltpu.VMEM(table.shape, BF16),
            pltpu.VMEM((2, count, HALF_LONS), BF16),
            pltpu.VMEM((4, count, 128), F32),
            pltpu.VMEM((4, count, 128), F32),
            pltpu.VMEM((PAIRS * lats, 128), F32),
            pltpu.SemaphoreType.DMA((8,)),
        ],
        compiler_params=pltpu.CompilerParams(vmem_limit_bytes=52 * 2**20),
        name="fourier",
    )(slot_order, rows, jnp.asarray(table))


def legendre_kernel(lats, order_ref, table_ref, received, *refs):
    outs, (sent, symmetric, antisymmetric) = refs[:-3], refs[-3:]
    place = lax.axis_index("ang")
    column = lax.axis_index("rad")
    here_x, here_c = column // NC, column % NC
    slots, _, degrees = table_ref.shape
    half = NA // 2
    degree = lax.broadcasted_iota(jnp.int32, (64, degrees), 1)

    def upper_first(pair):
        return lax.shift_right_logical(order_ref[place * slots + pair * 2], 8)

    for step in range(slots // 4):
        at = slice(step * 2 * lats, (step + 1) * 2 * lats)
        pieces = [received[source, at, :].astype(F32) for source in range(2 * half)]
        for pair in range(step * 2, step * 2 + 2):
            rows = slice(pair % 2 * lats, (pair % 2 + 1) * lats)
            north = jnp.concatenate([piece[rows] for piece in pieces[:half]], axis=0)
            mirrored = jnp.concatenate([piece[rows] for piece in pieces[half:][::-1]], axis=0)
            symmetric[pair] = (north + mirrored).astype(BF16).T
            antisymmetric[pair] = (north - mirrored).astype(BF16).T

    for pair in range(slots // 2):
        first = order_ref[place * slots + pair * 2]
        lower = jnp.where(first >= ORDERS // 2, ORDERS - 1 - first, first)
        chosen = []
        for which, order in enumerate((lower, ORDERS - 1 - lower)):
            begin = which * (degrees // 2)
            wanted = pl.ds(pl.multiple_of((order & 1) * 64, 64), 64)
            both = jnp.concatenate([symmetric[pair, wanted], antisymmetric[pair, wanted]], axis=0)
            result = jnp.dot(both, table_ref[pair * 2 + (upper_first(pair) ^ which), :, begin:], preferred_element_type=F32)
            here = degree[:, begin:]
            kept = jnp.where(((here ^ order) & 1) == 0, result[:64], result[64:])
            chosen.append(jnp.where(here >= order, kept, 0.0).astype(BF16))
        out_at = slice(pair * 64, pair * 64 + 64)
        for block in range(NR):
            left = chosen[0][:, block * 64 : block * 64 + 64]
            right = jnp.zeros_like(left)
            if block * 64 >= degrees // 2:
                right = chosen[1][:, block * 64 - degrees // 2 : block * 64 - degrees // 2 + 64]
            step_x = (block // NC - here_x) & (NX - 1)
            sent[step_x * NC + ((block % NC) ^ here_c), out_at, :] = jnp.concatenate([left, right], axis=1)
    outs = iter(outs)
    for step_x in range(NX):
        if step_x in DIRECT:
            for step_c in range(NC):
                next(outs)[...] = sent[step_x * NC + step_c]
        else:
            next(outs)[...] = sent[step_x * NC : step_x * NC + NC]


def legendre_stage(slot_order, received, legendre, lats):
    slots, _, _ = legendre.shape
    rows = slots * 32
    shapes = []
    for step_x in range(NX):
        if step_x in DIRECT:
            shapes += [jax.ShapeDtypeStruct((rows, 128), BF16)] * NC
        else:
            shapes.append(jax.ShapeDtypeStruct((NC, rows, 128), BF16))
    sent = pl.pallas_call(
        functools.partial(legendre_kernel, lats),
        out_shape=shapes,
        in_specs=[SMEM, VMEM, VMEM],
        out_specs=[VMEM] * len(shapes),
        scratch_shapes=[
            pltpu.VMEM((NR, slots * 32, 128), BF16),
            pltpu.VMEM((slots // 2, 128, legendre.shape[1]), BF16),
            pltpu.VMEM((slots // 2, 128, legendre.shape[1]), BF16),
        ],
        compiler_params=pltpu.CompilerParams(vmem_limit_bytes=24 * 2**20),
        name="legendre",
    )(slot_order, legendre, received)
    return sent


def solve_kernel(order_ref, inverse_ref, *refs):
    mine, others, (out_hbm, received, turned, solved, sems) = refs[:NX], refs[NX : 2 * NX], refs[-5:]
    place = lax.axis_index("ang")
    column = lax.axis_index("rad")
    here_x, here_c = column // NC, column % NC
    degrees = inverse_ref.shape[0]
    lines = solved.shape[1]
    pairs = lines // 8
    for index, step_x in enumerate(ARRIVALS):
        source = ((here_x - step_x) & (NX - 1)) * NC + here_c
        received[source] = mine[index][...] if step_x in DIRECT else mine[index][0]
        received[source ^ 1] = others[index][...]
    for pair in range(pairs):
        upper_first = lax.shift_right_logical(order_ref[(place * pairs + pair) * 2], 8)
        for part in range(4):
            at = slice(pair * 64 + part * 16, pair * 64 + part * 16 + 16)
            block = jnp.concatenate([received[source, at, :] for source in range(NR)], axis=0)
            block = block.T.astype(F32)
            for which in range(2):
                slot = pair * 2 + (upper_first ^ which)
                line = (part // 2) * (4 * pairs) + slot * 2 + part % 2
                turned[pl.ds(pl.multiple_of(line * LINE, 8), 64), :] = block[which * 64 : which * 64 + 64]

    def copy(group):
        at = pl.ds(pl.multiple_of(group * 8, 8), 8)
        return pltpu.make_async_copy(solved.at[group], out_hbm.at[:, at], sems.at[group])

    def solve(group, _):
        for degree in range(8):
            picked = turned[pl.ds(group * 8 + degree, lines, stride=LINE), :].astype(BF16)
            solved[group, :, degree, :] = lax.dot_general(
                picked, inverse_ref[group * 8 + degree], (((1,), (1,)), ((), ())), preferred_element_type=F32
            )
        copy(group).start()
        return 0

    lax.fori_loop(0, degrees // 8, solve, 0, unroll=8)
    for group in range(degrees // 8):
        copy(group).wait()


def solve_stage(slot_order, mine, others, inverses):
    degrees = inverses.shape[0]
    lines = others[0].shape[0] // 8
    operands = [slot_order, inverses, *(mine[i] for i in ARRIVALS), *(others[i] for i in ARRIVALS)]
    return pl.pallas_call(
        solve_kernel,
        out_shape=jax.ShapeDtypeStruct((lines, degrees, 128), F32),
        in_specs=[SMEM] + [VMEM] * (len(operands) - 1),
        out_specs=HBM,
        scratch_shapes=[
            pltpu.VMEM((NR, lines * 8, 128), BF16),
            pltpu.VMEM((lines * LINE, 128), F32),
            pltpu.VMEM((degrees // 8, lines, 8, 128), F32),
            pltpu.SemaphoreType.DMA((degrees // 8,)),
        ],
        compiler_params=PARAMS,
        name="solve",
    )(*operands)


def along_rad(sent):
    def move(part, step_x, step_c):
        pairs = [(a, (a // NC + step_x) % NX * NC + (a % NC ^ step_c)) for a in range(NX * NC)]
        return lax.ppermute(part, "rad", pairs)

    sent = iter(sent)
    mine, others = [], []
    for step_x in range(NX):
        part = next(sent)
        if step_x in DIRECT:
            mine.append(move(part, step_x, 0))
            others.append(move(next(sent), step_x, 1))
        else:
            mine.append(move(part, step_x, 0) if step_x else part)
            others.append(move(mine[-1][1], 0, 1))
    return mine, others


def body(grid_field, slot_order, legendre, inverses):
    fields, radii, lats, lons = grid_field.shape
    slots = legendre.shape[0]
    sent = fourier_stage(slot_order, grid_field.reshape(fields * radii * lats, lons), lats)
    received = lax.all_to_all(sent, "ang", split_axis=0, concat_axis=0)
    mine, others = along_rad(legendre_stage(slot_order, received, legendre, lats))
    spectrum = solve_stage(slot_order, mine, others, inverses)
    return spectrum.reshape(2, slots, fields, inverses.shape[0], 128)


def solution(mesh):
    placed = (P(None, "rad", "ang", None), P(), P("ang", None, None), P("rad", None, None))
    return jax.shard_map(
        body,
        mesh=mesh,
        in_specs=placed,
        out_specs=P(None, "ang", None, "rad", None),
        check_vma=False,
    )
```

```python
import functools
import math

import jax
import jax.numpy as jnp
import numpy as np
from jax import lax
from jax.experimental import pallas as pl
from jax.experimental.pallas import tpu as pltpu
from jax.sharding import PartitionSpec as P

LONS = 1536
HALF_LONS = LONS // 2
ORDERS = 512
PAIRS = ORDERS // 2
NA, NR = 32, 8
NX, NC = 4, 2
ARRIVALS = (0, 2, 1, 3)
DIRECT = (1, 3)
F32 = jnp.float32
BF16 = jnp.bfloat16
SMEM = pl.BlockSpec(memory_space=pltpu.SMEM)
VMEM = pl.BlockSpec(memory_space=pltpu.VMEM)
HBM = pl.BlockSpec(memory_space=pltpu.HBM)
PARAMS = pltpu.CompilerParams(vmem_limit_bytes=24 * 2**20)
CUTS = ((0, 128), (128, 384), (384, 768))
LINE = 72


def transform_tables():
    longitude = np.arange(HALF_LONS, dtype=np.int64)[:, None]
    halves = []
    for pairs in np.split(np.arange(PAIRS, dtype=np.int64), 2):
        tables = []
        for order in (2 * pairs, ORDERS - 1 - 2 * pairs):
            angle = (longitude * order[None, :] % LONS) * (2.0 * math.pi / LONS)
            columns = np.concatenate([np.cos(angle), -np.sin(angle)], axis=1)
            tables.append((columns / math.sqrt(LONS)).astype(np.float32).astype(BF16))
        halves.append(np.stack(tables))
    return np.stack(halves)


def fourier_kernel(lats, order_hbm, x_hbm, table_hbm, out_ref, order_ref, x_ref, table_ref, mixed, low, high, turned, sems):
    place = lax.axis_index("ang")
    columns = x_ref.shape[0] // lats
    pairs = PAIRS // NA
    order_copy = pltpu.make_async_copy(order_hbm, order_ref, sems.at[0])
    x_copies = [
        pltpu.make_async_copy(x_hbm.at[start:stop], x_ref.at[start:stop], sems.at[1 + index])
        for index, (start, stop) in enumerate(CUTS)
    ]
    table_copies = [
        [
            pltpu.make_async_copy(table_hbm.at[half, parity], table_ref.at[half, parity], sems.at[4 + half * 2 + parity])
            for parity in range(2)
        ]
        for half in range(2)
    ]
    for copy in (x_copies[0], *table_copies[0], *x_copies[1:], *table_copies[1], order_copy):
        copy.start()

    def turn(half, product, row):
        placed = jnp.where(place >= NA // 2, lats - 1 - row, row)
        picked = [product[part, pl.ds(row, columns, stride=lats), :] for part in range(4)]
        block = jnp.concatenate(picked, axis=0).T
        turned[pl.ds(half * 128 * lats + placed, 128, stride=lats), :] = block

    for index, (start, stop) in enumerate(CUTS):
        x_copies[index].wait()
        near = x_ref[start:stop, :HALF_LONS].astype(F32)
        far = x_ref[start:stop, HALF_LONS:].astype(F32)
        mixed[0, start:stop, :] = (near + far).astype(BF16)
        mixed[1, start:stop, :] = (near - far).astype(BF16)
        for parity in range(2):
            if start == 0:
                table_copies[0][parity].wait()
            result = jnp.dot(mixed[parity, start:stop, :], table_ref[0, parity], preferred_element_type=F32)
            for part in range(2):
                low[parity * 2 + part, start:stop, :] = result[:, part * 128 : part * 128 + 128]
    for parity in range(2):
        table_copies[1][parity].wait()
    share = lats // 2
    for index in range(2):
        result = jnp.dot(mixed[index], table_ref[1, index], preferred_element_type=F32)
        for part in range(2):
            high[index * 2 + part, : columns * lats, :] = result[:, part * 128 : part * 128 + 128]
        for row in range(index * share, (index + 1) * share):
            turn(0, low, row)

    def turn_high(row, _):
        turn(1, high, row)
        return 0

    lax.fori_loop(0, lats, turn_high, 0, unroll=24)
    order_copy.wait()

    def put(device, _):
        for local in range(0, pairs, 2):
            picked = []
            for offset in range(2):
                order = order_ref[(device * pairs + local + offset) * 2]
                pair = lax.shift_right_logical(order ^ ((order & 1) * (ORDERS - 1)), 1)
                picked.append(turned[pl.ds(pl.multiple_of(pair * lats, 8), lats), :])
            out_ref[device, local * lats : (local + 2) * lats, :] = jnp.concatenate(picked, axis=0).astype(BF16)
        return 0

    lax.fori_loop(0, NA, put, 0, unroll=8)


def fourier_stage(slot_order, rows, lats):
    table = transform_tables()
    count = rows.shape[0]
    return pl.pallas_call(
        functools.partial(fourier_kernel, lats),
        out_shape=jax.ShapeDtypeStruct((NA, PAIRS // NA * lats, 128), BF16),
        in_specs=[HBM, HBM, HBM],
        out_specs=VMEM,
        scratch_shapes=[
            pltpu.SMEM(slot_order.shape, jnp.int32),
            pltpu.VMEM(rows.shape, BF16),
            pltpu.VMEM(table.shape, BF16),
            pltpu.VMEM((2, count, HALF_LONS), BF16),
            pltpu.VMEM((4, count + lats, 128), F32),
            pltpu.VMEM((4, count + lats, 128), F32),
            pltpu.VMEM((PAIRS * lats + lats, 128), F32),
            pltpu.SemaphoreType.DMA((8,)),
        ],
        compiler_params=pltpu.CompilerParams(vmem_limit_bytes=52 * 2**20),
        name="fourier",
    )(slot_order, rows, jnp.asarray(table))


def legendre_kernel(lats, order_ref, table_ref, received, *refs):
    outs, (sent, symmetric, antisymmetric) = refs[:-3], refs[-3:]
    place = lax.axis_index("ang")
    column = lax.axis_index("rad")
    here_x, here_c = column // NC, column % NC
    slots, _, degrees = table_ref.shape
    half = NA // 2
    degree = lax.broadcasted_iota(jnp.int32, (64, degrees), 1)

    def upper_first(pair):
        return lax.shift_right_logical(order_ref[place * slots + pair * 2], 8)

    for step in range(slots // 4):
        at = slice(step * 2 * lats, (step + 1) * 2 * lats)
        pieces = [received[source, at, :].astype(F32) for source in range(2 * half)]
        for pair in range(step * 2, step * 2 + 2):
            rows = slice(pair % 2 * lats, (pair % 2 + 1) * lats)
            north = jnp.concatenate([piece[rows] for piece in pieces[:half]], axis=0)
            mirrored = jnp.concatenate([piece[rows] for piece in pieces[half:][::-1]], axis=0)
            symmetric[pair] = (north + mirrored).astype(BF16).T
            antisymmetric[pair] = (north - mirrored).astype(BF16).T

    for pair in range(slots // 2):
        first = order_ref[place * slots + pair * 2]
        lower = jnp.where(first >= ORDERS // 2, ORDERS - 1 - first, first)
        chosen = []
        for which, order in enumerate((lower, ORDERS - 1 - lower)):
            begin = which * (degrees // 2)
            wanted = pl.ds(pl.multiple_of((order & 1) * 64, 64), 64)
            both = jnp.concatenate([symmetric[pair, wanted], antisymmetric[pair, wanted]], axis=0)
            result = jnp.dot(both, table_ref[pair * 2 + (upper_first(pair) ^ which), :, begin:], preferred_element_type=F32)
            here = degree[:, begin:]
            kept = jnp.where(((here ^ order) & 1) == 0, result[:64], result[64:])
            chosen.append(jnp.where(here >= order, kept, 0.0).astype(BF16))
        out_at = slice(pair * 64, pair * 64 + 64)
        for block in range(NR):
            left = chosen[0][:, block * 64 : block * 64 + 64]
            right = jnp.zeros_like(left)
            if block * 64 >= degrees // 2:
                right = chosen[1][:, block * 64 - degrees // 2 : block * 64 - degrees // 2 + 64]
            step_x = (block // NC - here_x) & (NX - 1)
            sent[step_x * NC + ((block % NC) ^ here_c), out_at, :] = jnp.concatenate([left, right], axis=1)
    outs = iter(outs)
    for step_x in range(NX):
        if step_x in DIRECT:
            for step_c in range(NC):
                next(outs)[...] = sent[step_x * NC + step_c]
        else:
            next(outs)[...] = sent[step_x * NC : step_x * NC + NC]


def legendre_stage(slot_order, received, legendre, lats):
    slots, _, _ = legendre.shape
    rows = slots * 32
    shapes = []
    for step_x in range(NX):
        if step_x in DIRECT:
            shapes += [jax.ShapeDtypeStruct((rows, 128), BF16)] * NC
        else:
            shapes.append(jax.ShapeDtypeStruct((NC, rows, 128), BF16))
    sent = pl.pallas_call(
        functools.partial(legendre_kernel, lats),
        out_shape=shapes,
        in_specs=[SMEM, VMEM, VMEM],
        out_specs=[VMEM] * len(shapes),
        scratch_shapes=[
            pltpu.VMEM((NR, slots * 32, 128), BF16),
            pltpu.VMEM((slots // 2, 128, legendre.shape[1]), BF16),
            pltpu.VMEM((slots // 2, 128, legendre.shape[1]), BF16),
        ],
        compiler_params=pltpu.CompilerParams(vmem_limit_bytes=24 * 2**20),
        name="legendre",
    )(slot_order, legendre, received)
    return sent


def solve_kernel(order_ref, inverse_ref, *refs):
    mine, others, (out_hbm, received, turned, solved, sems) = refs[:NX], refs[NX : 2 * NX], refs[-5:]
    place = lax.axis_index("ang")
    column = lax.axis_index("rad")
    here_x, here_c = column // NC, column % NC
    degrees = inverse_ref.shape[0]
    lines = solved.shape[1]
    pairs = lines // 8
    for index, step_x in enumerate(ARRIVALS):
        source = ((here_x - step_x) & (NX - 1)) * NC + here_c
        received[source] = mine[index][...] if step_x in DIRECT else mine[index][0]
        received[source ^ 1] = others[index][...]
    for pair in range(pairs):
        upper_first = lax.shift_right_logical(order_ref[(place * pairs + pair) * 2], 8)
        for part in range(4):
            at = slice(pair * 64 + part * 16, pair * 64 + part * 16 + 16)
            block = jnp.concatenate([received[source, at, :] for source in range(NR)], axis=0)
            block = block.T.astype(F32)
            for which in range(2):
                slot = pair * 2 + (upper_first ^ which)
                line = (part // 2) * (4 * pairs) + slot * 2 + part % 2
                turned[pl.ds(pl.multiple_of(line * LINE, 8), 64), :] = block[which * 64 : which * 64 + 64]

    def copy(group):
        at = pl.ds(pl.multiple_of(group * 8, 8), 8)
        return pltpu.make_async_copy(solved.at[group], out_hbm.at[:, at], sems.at[group])

    def solve(group, _):
        for degree in range(8):
            picked = turned[pl.ds(group * 8 + degree, lines, stride=LINE), :].astype(BF16)
            solved[group, :, degree, :] = lax.dot_general(
                picked, inverse_ref[group * 8 + degree], (((1,), (1,)), ((), ())), preferred_element_type=F32
            )
        copy(group).start()
        return 0

    lax.fori_loop(0, degrees // 8, solve, 0, unroll=8)
    for group in range(degrees // 8):
        copy(group).wait()


def solve_stage(slot_order, mine, others, inverses):
    degrees = inverses.shape[0]
    lines = others[0].shape[0] // 8
    operands = [slot_order, inverses, *(mine[i] for i in ARRIVALS), *(others[i] for i in ARRIVALS)]
    return pl.pallas_call(
        solve_kernel,
        out_shape=jax.ShapeDtypeStruct((lines, degrees, 128), F32),
        in_specs=[SMEM] + [VMEM] * (len(operands) - 1),
        out_specs=HBM,
        scratch_shapes=[
            pltpu.VMEM((NR, lines * 8, 128), BF16),
            pltpu.VMEM((lines * LINE + LINE, 128), F32),
            pltpu.VMEM((degrees // 8, lines, 8, 128), F32),
            pltpu.SemaphoreType.DMA((degrees // 8,)),
        ],
        compiler_params=PARAMS,
        name="solve",
    )(*operands)


def along_rad(sent):
    def move(part, step_x, step_c):
        pairs = [(a, (a // NC + step_x) % NX * NC + (a % NC ^ step_c)) for a in range(NX * NC)]
        return lax.ppermute(part, "rad", pairs)

    sent = iter(sent)
    mine, others = [], []
    for step_x in range(NX):
        part = next(sent)
        if step_x in DIRECT:
            mine.append(move(part, step_x, 0))
            others.append(move(next(sent), step_x, 1))
        else:
            mine.append(move(part, step_x, 0) if step_x else part)
            others.append(move(mine[-1][1], 0, 1))
    return mine, others


def body(grid_field, slot_order, legendre, inverses):
    fields, radii, lats, lons = grid_field.shape
    slots = legendre.shape[0]
    sent = fourier_stage(slot_order, grid_field.reshape(fields * radii * lats, lons), lats)
    received = lax.all_to_all(sent, "ang", split_axis=0, concat_axis=0)
    mine, others = along_rad(legendre_stage(slot_order, received, legendre, lats))
    spectrum = solve_stage(slot_order, mine, others, inverses)
    return spectrum.reshape(2, slots, fields, inverses.shape[0], 128)


def solution(mesh):
    placed = (P(None, "rad", "ang", None), P(), P("ang", None, None), P("rad", None, None))
    return jax.shard_map(
        body,
        mesh=mesh,
        in_specs=placed,
        out_specs=P(None, "ang", None, "rad", None),
        check_vma=False,
    )
```

```python
import functools
import math

import jax
import jax.numpy as jnp
import numpy as np
from jax import lax
from jax.experimental import pallas as pl
from jax.experimental.pallas import tpu as pltpu
from jax.sharding import PartitionSpec as P

LONS = 1536
HALF_LONS = LONS // 2
ORDERS = 512
PAIRS = ORDERS // 2
NA, NR = 32, 8
NX, NC = 4, 2
ARRIVALS = (0, 2, 1, 3)
DIRECT = (1, 3)
F32 = jnp.float32
BF16 = jnp.bfloat16
SMEM = pl.BlockSpec(memory_space=pltpu.SMEM)
VMEM = pl.BlockSpec(memory_space=pltpu.VMEM)
HBM = pl.BlockSpec(memory_space=pltpu.HBM)
PARAMS = pltpu.CompilerParams(vmem_limit_bytes=24 * 2**20)
CUTS = ((0, 128), (128, 384), (384, 768))
LINE = 72


def transform_tables():
    longitude = np.arange(HALF_LONS, dtype=np.int64)[:, None]
    halves = []
    for pairs in np.split(np.arange(PAIRS, dtype=np.int64), 2):
        tables = []
        for order in (2 * pairs, ORDERS - 1 - 2 * pairs):
            angle = (longitude * order[None, :] % LONS) * (2.0 * math.pi / LONS)
            columns = np.concatenate([np.cos(angle), -np.sin(angle)], axis=1)
            tables.append((columns / math.sqrt(LONS)).astype(np.float32).astype(BF16))
        halves.append(np.stack(tables))
    return np.stack(halves)


def fourier_kernel(lats, order_hbm, x_hbm, table_hbm, out_ref, order_ref, x_ref, table_ref, mixed, low, high, turned, sems):
    place = lax.axis_index("ang")
    columns = x_ref.shape[0] // lats
    pairs = PAIRS // NA
    order_copy = pltpu.make_async_copy(order_hbm, order_ref, sems.at[0])
    x_copies = [
        pltpu.make_async_copy(x_hbm.at[start:stop], x_ref.at[start:stop], sems.at[1 + index])
        for index, (start, stop) in enumerate(CUTS)
    ]
    table_copies = [
        [
            pltpu.make_async_copy(table_hbm.at[half, parity], table_ref.at[half, parity], sems.at[4 + half * 2 + parity])
            for parity in range(2)
        ]
        for half in range(2)
    ]
    for copy in (x_copies[0], *table_copies[0], *x_copies[1:], *table_copies[1], order_copy):
        copy.start()

    def turn(half, product, row):
        placed = jnp.where(place >= NA // 2, lats - 1 - row, row)
        picked = [product[part, pl.ds(row, columns, stride=lats), :] for part in range(4)]
        block = jnp.concatenate(picked, axis=0).T
        turned[pl.ds(half * 128 * lats + placed, 128, stride=lats), :] = block

    for index, (start, stop) in enumerate(CUTS):
        x_copies[index].wait()
        near = x_ref[start:stop, :HALF_LONS].astype(F32)
        far = x_ref[start:stop, HALF_LONS:].astype(F32)
        mixed[0, start:stop, :] = (near + far).astype(BF16)
        mixed[1, start:stop, :] = (near - far).astype(BF16)
        for parity in range(2):
            if start == 0:
                table_copies[0][parity].wait()
            result = jnp.dot(mixed[parity, start:stop, :], table_ref[0, parity], preferred_element_type=F32)
            for part in range(2):
                low[parity * 2 + part, start:stop, :] = result[:, part * 128 : part * 128 + 128]
    for parity in range(2):
        table_copies[1][parity].wait()
    share = lats // 2
    for index in range(2):
        result = jnp.dot(mixed[index], table_ref[1, index], preferred_element_type=F32)
        for part in range(2):
            high[index * 2 + part, : columns * lats, :] = result[:, part * 128 : part * 128 + 128]
        for row in range(index * share, (index + 1) * share):
            turn(0, low, row)

    def turn_high(row, _):
        turn(1, high, row)
        return 0

    lax.fori_loop(0, lats, turn_high, 0, unroll=24)
    order_copy.wait()

    def put(device, _):
        for local in range(0, pairs, 2):
            picked = []
            for offset in range(2):
                order = order_ref[(device * pairs + local + offset) * 2]
                pair = lax.shift_right_logical(order ^ ((order & 1) * (ORDERS - 1)), 1)
                picked.append(turned[pl.ds(pl.multiple_of(pair * lats, 8), lats), :])
            out_ref[device, local * lats : (local + 2) * lats, :] = jnp.concatenate(picked, axis=0).astype(BF16)
        return 0

    lax.fori_loop(0, NA, put, 0, unroll=32)


def fourier_stage(slot_order, rows, lats):
    table = transform_tables()
    count = rows.shape[0]
    return pl.pallas_call(
        functools.partial(fourier_kernel, lats),
        out_shape=jax.ShapeDtypeStruct((NA, PAIRS // NA * lats, 128), BF16),
        in_specs=[HBM, HBM, HBM],
        out_specs=VMEM,
        scratch_shapes=[
            pltpu.SMEM(slot_order.shape, jnp.int32),
            pltpu.VMEM(rows.shape, BF16),
            pltpu.VMEM(table.shape, BF16),
            pltpu.VMEM((2, count, HALF_LONS), BF16),
            pltpu.VMEM((4, count + lats, 128), F32),
            pltpu.VMEM((4, count + lats, 128), F32),
            pltpu.VMEM((PAIRS * lats + lats, 128), F32),
            pltpu.SemaphoreType.DMA((8,)),
        ],
        compiler_params=pltpu.CompilerParams(vmem_limit_bytes=52 * 2**20),
        name="fourier",
    )(slot_order, rows, jnp.asarray(table))


def legendre_kernel(lats, order_ref, table_ref, received, *refs):
    outs, (sent, symmetric, antisymmetric) = refs[:-3], refs[-3:]
    place = lax.axis_index("ang")
    column = lax.axis_index("rad")
    here_x, here_c = column // NC, column % NC
    slots, _, degrees = table_ref.shape
    half = NA // 2
    degree = lax.broadcasted_iota(jnp.int32, (64, degrees), 1)

    def upper_first(pair):
        return lax.shift_right_logical(order_ref[place * slots + pair * 2], 8)

    for step in range(slots // 4):
        at = slice(step * 2 * lats, (step + 1) * 2 * lats)
        pieces = [received[source, at, :].astype(F32) for source in range(2 * half)]
        for pair in range(step * 2, step * 2 + 2):
            rows = slice(pair % 2 * lats, (pair % 2 + 1) * lats)
            north = jnp.concatenate([piece[rows] for piece in pieces[:half]], axis=0)
            mirrored = jnp.concatenate([piece[rows] for piece in pieces[half:][::-1]], axis=0)
            symmetric[pair] = (north + mirrored).astype(BF16).T
            antisymmetric[pair] = (north - mirrored).astype(BF16).T

    for pair in range(slots // 2):
        first = order_ref[place * slots + pair * 2]
        lower = jnp.where(first >= ORDERS // 2, ORDERS - 1 - first, first)
        chosen = []
        for which, order in enumerate((lower, ORDERS - 1 - lower)):
            begin = which * (degrees // 2)
            wanted = pl.ds(pl.multiple_of((order & 1) * 64, 64), 64)
            both = jnp.concatenate([symmetric[pair, wanted], antisymmetric[pair, wanted]], axis=0)
            result = jnp.dot(both, table_ref[pair * 2 + (upper_first(pair) ^ which), :, begin:], preferred_element_type=F32)
            here = degree[:, begin:]
            kept = jnp.where(((here ^ order) & 1) == 0, result[:64], result[64:])
            chosen.append(jnp.where(here >= order, kept, 0.0).astype(BF16))
        out_at = slice(pair * 64, pair * 64 + 64)
        for block in range(NR):
            left = chosen[0][:, block * 64 : block * 64 + 64]
            right = jnp.zeros_like(left)
            if block * 64 >= degrees // 2:
                right = chosen[1][:, block * 64 - degrees // 2 : block * 64 - degrees // 2 + 64]
            step_x = (block // NC - here_x) & (NX - 1)
            sent[step_x * NC + ((block % NC) ^ here_c), out_at, :] = jnp.concatenate([left, right], axis=1)
    outs = iter(outs)
    for step_x in range(NX):
        if step_x in DIRECT:
            for step_c in range(NC):
                next(outs)[...] = sent[step_x * NC + step_c]
        else:
            next(outs)[...] = sent[step_x * NC : step_x * NC + NC]


def legendre_stage(slot_order, received, legendre, lats):
    slots, _, _ = legendre.shape
    rows = slots * 32
    shapes = []
    for step_x in range(NX):
        if step_x in DIRECT:
            shapes += [jax.ShapeDtypeStruct((rows, 128), BF16)] * NC
        else:
            shapes.append(jax.ShapeDtypeStruct((NC, rows, 128), BF16))
    sent = pl.pallas_call(
        functools.partial(legendre_kernel, lats),
        out_shape=shapes,
        in_specs=[SMEM, VMEM, VMEM],
        out_specs=[VMEM] * len(shapes),
        scratch_shapes=[
            pltpu.VMEM((NR, slots * 32, 128), BF16),
            pltpu.VMEM((slots // 2, 128, legendre.shape[1]), BF16),
            pltpu.VMEM((slots // 2, 128, legendre.shape[1]), BF16),
        ],
        compiler_params=pltpu.CompilerParams(vmem_limit_bytes=24 * 2**20),
        name="legendre",
    )(slot_order, legendre, received)
    return sent


def solve_kernel(order_ref, inverse_ref, *refs):
    mine, others, (out_hbm, received, turned, solved, sems) = refs[:NX], refs[NX : 2 * NX], refs[-5:]
    place = lax.axis_index("ang")
    column = lax.axis_index("rad")
    here_x, here_c = column // NC, column % NC
    degrees = inverse_ref.shape[0]
    lines = solved.shape[1]
    pairs = lines // 8
    for index, step_x in enumerate(ARRIVALS):
        source = ((here_x - step_x) & (NX - 1)) * NC + here_c
        received[source] = mine[index][...] if step_x in DIRECT else mine[index][0]
        received[source ^ 1] = others[index][...]
    for pair in range(pairs):
        upper_first = lax.shift_right_logical(order_ref[(place * pairs + pair) * 2], 8)
        for part in range(4):
            at = slice(pair * 64 + part * 16, pair * 64 + part * 16 + 16)
            block = jnp.concatenate([received[source, at, :] for source in range(NR)], axis=0)
            block = block.T.astype(F32)
            for which in range(2):
                slot = pair * 2 + (upper_first ^ which)
                line = (part // 2) * (4 * pairs) + slot * 2 + part % 2
                turned[pl.ds(pl.multiple_of(line * LINE, 8), 64), :] = block[which * 64 : which * 64 + 64]

    def copy(group):
        at = pl.ds(pl.multiple_of(group * 8, 8), 8)
        return pltpu.make_async_copy(solved.at[group], out_hbm.at[:, at], sems.at[group])

    def solve(group, _):
        for degree in range(8):
            picked = turned[pl.ds(group * 8 + degree, lines, stride=LINE), :].astype(BF16)
            solved[group, :, degree, :] = lax.dot_general(
                picked, inverse_ref[group * 8 + degree], (((1,), (1,)), ((), ())), preferred_element_type=F32
            )
        copy(group).start()
        return 0

    lax.fori_loop(0, degrees // 8, solve, 0, unroll=8)
    for group in range(degrees // 8):
        copy(group).wait()


def solve_stage(slot_order, mine, others, inverses):
    degrees = inverses.shape[0]
    lines = others[0].shape[0] // 8
    operands = [slot_order, inverses, *(mine[i] for i in ARRIVALS), *(others[i] for i in ARRIVALS)]
    return pl.pallas_call(
        solve_kernel,
        out_shape=jax.ShapeDtypeStruct((lines, degrees, 128), F32),
        in_specs=[SMEM] + [VMEM] * (len(operands) - 1),
        out_specs=HBM,
        scratch_shapes=[
            pltpu.VMEM((NR, lines * 8, 128), BF16),
            pltpu.VMEM((lines * LINE + LINE, 128), F32),
            pltpu.VMEM((degrees // 8, lines, 8, 128), F32),
            pltpu.SemaphoreType.DMA((degrees // 8,)),
        ],
        compiler_params=PARAMS,
        name="solve",
    )(*operands)


def along_rad(sent):
    def move(part, step_x, step_c):
        pairs = [(a, (a // NC + step_x) % NX * NC + (a % NC ^ step_c)) for a in range(NX * NC)]
        return lax.ppermute(part, "rad", pairs)

    sent = iter(sent)
    mine, others = [], []
    for step_x in range(NX):
        part = next(sent)
        if step_x in DIRECT:
            mine.append(move(part, step_x, 0))
            others.append(move(next(sent), step_x, 1))
        else:
            mine.append(move(part, step_x, 0) if step_x else part)
            others.append(move(mine[-1][1], 0, 1))
    return mine, others


def body(grid_field, slot_order, legendre, inverses):
    fields, radii, lats, lons = grid_field.shape
    slots = legendre.shape[0]
    sent = fourier_stage(slot_order, grid_field.reshape(fields * radii * lats, lons), lats)
    received = lax.all_to_all(sent, "ang", split_axis=0, concat_axis=0)
    mine, others = along_rad(legendre_stage(slot_order, received, legendre, lats))
    spectrum = solve_stage(slot_order, mine, others, inverses)
    return spectrum.reshape(2, slots, fields, inverses.shape[0], 128)


def solution(mesh):
    placed = (P(None, "rad", "ang", None), P(), P("ang", None, None), P("rad", None, None))
    return jax.shard_map(
        body,
        mesh=mesh,
        in_specs=placed,
        out_specs=P(None, "ang", None, "rad", None),
        check_vma=False,
    )
```
